32 devices in a mesh: wide: 8 (over y, x, core), narrow: 4 (over z).
Axes of the slice: x: 2, y: 2, z: 4, core: 2. Of those that a mesh axis runs over, the one named last changes fastest.
Arguments:
- tokens: bfloat16 [128, 128, 1536], P('wide'), may hold values from -8 to 8
- ln_gain: bfloat16 [1536], replicated, may hold values from 0.3984375 to 1.59375
- gate_weight: bfloat16 [1536, 8960], P(None, 'narrow'), may hold values from -0.15625 to 0.15625
- up_weight: bfloat16 [1536, 8960], P(None, 'narrow'), may hold values from -0.15625 to 0.15625
- down_weight: bfloat16 [8960, 1536], P('narrow'), may hold values from -0.0625 to 0.0625
- out_gain: bfloat16 [1536], replicated, may hold values from 0.25 to 1.75
- shard_ids: int32 [128], P('wide'), may hold values from 0 to 7, as said below
- slab_old: bfloat16 [65536, 1536], P(('wide', 'narrow')), may hold values from -8 to 8
- queries: bfloat16 [8, 64, 1536], P('wide'), may hold values from -12 to 12
- positives: int32 [8, 64], P('wide'), may hold values from 0 to 65663
- owners: int32 [4], replicated, may hold values from 0 to 7
Outputs:
- index_new: bfloat16 [8, 8, 4, 1536], P('wide', 'narrow')
- losses: float32 [4, 64], replicated
The draws below stay inside these ranges and needn't reach their ends.
Inputs may be any that keep to these rules, and one draw needn't show every extreme that they name: `shard_ids`: among the 16 passages of one index of wide at most 4 have the same shard id; in every draw one shard id is held by exactly 4 passages of every index of wide.
All inputs are finite; a program needn't handle non-finite values.
Results may differ from the reference program's by a relative error of at most 0.0029.
Values may be sent and summed in bfloat16 or wider, within the bound.
A program may use at most 128 MiB of HBM per device.

```python
import math
import jax
import jax.numpy as jnp
from jax import lax

D = 1536
FF = 8960
SEQ = 128
PASS = 16
QB = 64
STEPS = 4
CAP = 4
NEW_TOTAL = 128
OLD_TOTAL = 65536
N_WIDE = 8


def block_patterns(key):
    return jnp.where(jax.random.bernoulli(jax.random.fold_in(key, 9), 0.5, (N_WIDE, D)), 1.0, -1.0).astype(jnp.float32)


def draw_tokens(key, part):
    k_topic = jax.random.fold_in(key, 21)
    k_noise = jax.random.fold_in(key, 22)
    k_jitter = jax.random.fold_in(key, 24)
    k_place = jax.random.fold_in(key, 10)
    columns = jnp.arange(D, dtype=jnp.float32) / D
    patterns = block_patterns(key)
    ramp = 0.8 + 0.6 * columns
    topic = jax.random.normal(k_topic, (NEW_TOTAL, 1, D), jnp.float32)
    noise = jax.random.normal(k_noise, (NEW_TOTAL, SEQ, D), jnp.float32)
    values = topic * ramp + noise
    jitter = 0.3 * jax.random.normal(k_jitter, (N_WIDE, SEQ, D), jnp.float32)
    planted = 2.0 * patterns[:, None, :] + jitter
    chosen = jax.random.randint(k_place, (N_WIDE,), 0, PASS)
    marked = (jnp.arange(PASS, dtype=jnp.int32)[None, :] == chosen[:, None])[:, :, None, None]
    values = jnp.where(marked, planted[:, None, :, :], values.reshape(N_WIDE, PASS, SEQ, D))
    return jnp.clip(values, -8.0, 8.0).reshape(NEW_TOTAL, SEQ, D).astype(jnp.bfloat16)


def draw_shard_ids(key, part):
    full = jax.random.randint(jax.random.fold_in(key, 3), (), 0, N_WIDE)
    others = jnp.arange((N_WIDE - 1) * CAP, dtype=jnp.int32) // CAP
    others = others + (others >= full).astype(jnp.int32)
    keys = jax.random.split(jax.random.fold_in(key, 4), N_WIDE)

    def block(block_key):
        first_key, second_key = jax.random.split(block_key)
        chosen = jax.random.permutation(first_key, others)[:PASS - CAP]
        rows = jnp.concatenate([jnp.full((CAP,), full, jnp.int32), chosen])
        return jax.random.permutation(second_key, rows)
    return jax.vmap(block)(keys).reshape(NEW_TOTAL).astype(jnp.int32)


def draw_slab_old(key, part):
    k_base = jax.random.fold_in(key, 11)
    rows = jnp.arange(OLD_TOTAL, dtype=jnp.float32) / OLD_TOTAL
    ramp = (0.94 + 0.12 * rows)[:, None]
    values = jax.random.normal(k_base, (OLD_TOTAL, D), jnp.float32) * ramp
    return jnp.clip(values, -8.0, 8.0).astype(jnp.bfloat16)


def draw_queries(key, part):
    k_base = jax.random.fold_in(key, 31)
    row_ids = jnp.arange(N_WIDE * QB, dtype=jnp.int32)
    patterns = block_patterns(key)
    matched = patterns[row_ids // 8 % N_WIDE] * 4.0
    to_new = (row_ids % 8 == 4)[:, None]
    values = jax.random.normal(k_base, (N_WIDE * QB, D), jnp.float32) * 6.0
    values = jnp.where(to_new, matched, values)
    return jnp.clip(values, -12.0, 12.0).reshape(N_WIDE, QB, D).astype(jnp.bfloat16)


def touch_ends(array, rng, smallest, high):
    spot = [jax.random.randint(jax.random.fold_in(rng, axis), (), 0, length) for axis, length in enumerate(array.shape)]
    widest = array.shape.index(max(array.shape))
    next_to = spot[:widest] + [(spot[widest] + 1) % array.shape[widest]] + spot[widest + 1:]
    return array.at[tuple(spot)].set(smallest).at[tuple(next_to)].set(high)


def block_levels(rng, shape, cuts, smallest, high):
    loudness, own = 1.0, jax.random.fold_in(rng, 6)
    for dim, shards_of in cuts:
        steps = jnp.exp(jax.random.uniform(jax.random.fold_in(own, dim), (shards_of,), jnp.float32, smallest / len(cuts), high / len(cuts)))
        loudness = loudness * jnp.repeat(steps, shape[dim] // shards_of).reshape([-1 if axis == dim else 1 for axis in range(len(shape))])
    return loudness


def bell_draw(own_key, extent, deviation, limit, cuts=(), kind=jnp.bfloat16):
    drawn = deviation * jax.random.normal(own_key, extent, jnp.float32)
    if cuts:
        drawn = drawn * block_levels(own_key, extent, cuts, -0.22, 0.18)
    return jnp.clip(drawn, -limit, limit).astype(kind)


def setup_inputs(seed: int = 0) -> dict:
    streams_of = jax.random.split(jax.random.key(seed), 12)
    tokens = draw_tokens(jax.random.fold_in(streams_of[11], 71), 0)
    ln_gain = jnp.clip(1.0 + 0.12 * jax.random.normal(streams_of[1], (D,), jnp.float32), 0.3984375, 1.59375).astype(jnp.bfloat16)
    gate_weight = bell_draw(streams_of[2], (D, FF), D ** -0.5, 0.15625, ((1, 4),))
    up_weight = bell_draw(streams_of[3], (D, FF), D ** -0.5, 0.15625, ((1, 4),))
    down_weight = bell_draw(streams_of[4], (FF, D), FF ** -0.5, 0.0625, ((0, 4),))
    out_gain = jnp.clip(1.0 + 0.15 * jax.random.normal(streams_of[5], (D,), jnp.float32), 0.25, 1.75).astype(jnp.bfloat16)
    shard_ids = draw_shard_ids(jax.random.fold_in(streams_of[11], 71), 0)
    slab_old = draw_slab_old(jax.random.fold_in(streams_of[11], 71), 0)
    queries = draw_queries(jax.random.fold_in(streams_of[11], 71), 0)
    positives = touch_ends(jax.random.randint(streams_of[9], (N_WIDE, QB), 0, OLD_TOTAL + NEW_TOTAL), jax.random.fold_in(streams_of[9], 1), 0, (OLD_TOTAL + NEW_TOTAL) - 1).astype(jnp.int32)
    owners = touch_ends(jax.random.randint(streams_of[10], (STEPS,), 0, N_WIDE), jax.random.fold_in(streams_of[10], 1), 0, N_WIDE - 1).astype(jnp.int32)
    return {"tokens": tokens, "ln_gain": ln_gain, "gate_weight": gate_weight, "up_weight": up_weight, "down_weight": down_weight, "out_gain": out_gain, "shard_ids": shard_ids, "slab_old": slab_old, "queries": queries, "positives": positives, "owners": owners}


EPS = 1e-06

def rms_scale(values):
    return lax.rsqrt(lax.optimization_barrier(jnp.mean(values * values, axis=-1, keepdims=True)) + EPS)

def reference(tokens, ln_gain, gate_weight, up_weight, down_weight, out_gain, shard_ids, slab_old, queries, positives, owners):
    gain_in = ln_gain.astype(jnp.float32)
    gain_out = out_gain.astype(jnp.float32)

    def encode(group):
        values = group.astype(jnp.float32)
        normed = (values * rms_scale(values) * gain_in).astype(jnp.bfloat16).reshape(PASS * SEQ, D)
        gate = jnp.dot(normed, gate_weight, preferred_element_type=jnp.float32)
        upward = jnp.dot(normed, up_weight, preferred_element_type=jnp.float32)
        hidden = (jax.nn.silu(gate) * upward).astype(jnp.bfloat16)
        mixed = jnp.dot(hidden, down_weight, preferred_element_type=jnp.float32).reshape(PASS, SEQ, D)
        pooled = lax.optimization_barrier(jnp.mean(values + mixed, axis=1))
        return (pooled * rms_scale(pooled) * gain_out).astype(jnp.bfloat16)
    embeddings = lax.map(encode, tokens.reshape(N_WIDE, PASS, SEQ, D))
    positions = jnp.arange(PASS, dtype=jnp.int32)
    earlier = positions[:, None] > positions[None, :]

    def place(shards, rows):
        same = shards[:, None] == shards[None, :]
        rank = lax.optimization_barrier(jnp.sum((earlier & same).astype(jnp.int32), axis=1))
        slots = (shards * CAP + rank).astype(jnp.int32)
        empty = jnp.zeros((N_WIDE * CAP, D), jnp.bfloat16)
        return empty.at[slots].set(rows).reshape(N_WIDE, CAP, D)
    placed = jax.vmap(place)(shard_ids.reshape(N_WIDE, PASS), embeddings)
    index_new = jnp.transpose(placed, (1, 0, 2, 3))
    fresh = embeddings.reshape(NEW_TOTAL, D)
    scale = 1.0 / math.sqrt(D)
    contract = (((1,), (1,)), ((), ()))

    def step_loss(owner):
        block = queries[owner]
        positive = positives[owner]
        old_scores = lax.dot_general(block, slab_old, contract, preferred_element_type=jnp.float32) * scale
        new_scores = lax.dot_general(block, fresh, contract, preferred_element_type=jnp.float32) * scale
        scores = jnp.concatenate([old_scores, new_scores], axis=1)
        top = lax.optimization_barrier(jnp.max(scores, axis=1))
        total = lax.optimization_barrier(jnp.sum(jnp.exp(scores - top[:, None]), axis=1))
        picked = jnp.take_along_axis(scores, positive[:, None].astype(jnp.int32), axis=1)[:, 0]
        return top + jnp.log(total) - picked
    losses = lax.map(step_loss, owners)
    return (index_new, losses)
```

```python
import functools
import math

import jax
import jax.numpy as jnp
from jax import lax
from jax.experimental import pallas as pl
from jax.experimental.pallas import tpu as pltpu
from jax.sharding import PartitionSpec as P

EPS = 1e-06
MESH = pl.DeviceIdType.MESH
CHUNK = 256
ROWS = 256
SPLIT = 4
LOADS = 4
MSG = 16


def kernel(
    dims,
    tokens_ref,
    gain_ref,
    gate_ref,
    up_ref,
    down_ref,
    out_gain_ref,
    place_ref,
    slab_ref,
    queries_ref,
    positives_ref,
    owners_ref,
    index_ref,
    losses_ref,
    x_ref,
    gate_v,
    up_v,
    down_v,
    slab_v,
    q_all,
    p_all,
    blocks,
    hidden_sum,
    token_mean,
    total,
    part,
    part_in,
    messages,
    messages_in,
    stats,
    x_sem,
    w_sem,
    big_sem,
    own_sem,
    q_send,
    q_recv,
    p_send,
    p_recv,
    part_send,
    part_recv,
    msg_send,
    msg_recv,
    stat_send,
    stat_recv,
):
    passages, seq, wide_count, narrow_count, steps, block = dims
    width = tokens_ref.shape[1]
    units = gate_ref.shape[1]
    full, tail = units // CHUNK, units % CHUNK
    per = passages // narrow_count
    groups = 8 // per
    lanes = width // groups
    sources = wide_count // narrow_count
    devices = wide_count * narrow_count
    count = steps * block
    w = lax.axis_index("wide")
    n = lax.axis_index("narrow")
    me = w * narrow_count + n

    def token_copy(i):
        rows = pl.ds(pl.multiple_of(i * seq, seq), seq)
        return pltpu.make_async_copy(tokens_ref.at[rows, :], x_ref.at[rows, :], x_sem.at[i])

    def weight_copies(c):
        rows = pl.ds(pl.multiple_of(c * (width // LOADS), width // LOADS), width // LOADS)
        return (
            pltpu.make_async_copy(gate_ref.at[rows, :], gate_v.at[rows, :], w_sem.at[0, c]),
            pltpu.make_async_copy(up_ref.at[rows, :], up_v.at[rows, :], w_sem.at[1, c]),
        )

    down_copy = pltpu.make_async_copy(down_ref, down_v, big_sem.at[0])
    slab_copy = pltpu.make_async_copy(slab_ref, slab_v, big_sem.at[1])
    own_q = pltpu.make_async_copy(queries_ref, q_all.at[w], own_sem.at[0])
    own_p = pltpu.make_async_copy(positives_ref, p_all.at[w], own_sem.at[1])

    @pl.loop(0, passages)
    def _(i):
        token_copy(i).start()

    @pl.loop(0, LOADS)
    def _(c):
        for copy in weight_copies(c):
            copy.start()

    down_copy.start()
    slab_copy.start()
    own_q.start()
    own_p.start()

    barrier = pltpu.get_barrier_semaphore()

    @pl.loop(1, devices)
    def _(k):
        other = lax.rem(me + k, devices)
        pl.semaphore_signal(
            barrier,
            inc=1,
            device_id=(other // narrow_count, lax.rem(other, narrow_count)),
            device_id_type=MESH,
        )

    gain = gain_ref[...]

    @pl.loop(0, passages)
    def _(i):
        token_copy(i).wait()
        rows = pl.ds(pl.multiple_of(i * seq, seq), seq)
        values = x_ref[rows, :].astype(jnp.float32)
        scale = lax.rsqrt(jnp.mean(values * values, axis=1, keepdims=True) + EPS)
        token_mean[pl.ds(i, 1), :] = jnp.sum(values, axis=0, keepdims=True) * (1.0 / seq)
        x_ref[rows, :] = (values * scale * gain).astype(jnp.bfloat16)

    pl.semaphore_wait(barrier, devices - 1)

    def query_copies(owner, target):
        return (
            pltpu.make_async_remote_copy(
                src_ref=queries_ref,
                dst_ref=q_all.at[owner],
                send_sem=q_send.at[target],
                recv_sem=q_recv.at[owner],
                device_id=(target, n),
                device_id_type=MESH,
            ),
            pltpu.make_async_remote_copy(
                src_ref=positives_ref,
                dst_ref=p_all.at[owner],
                send_sem=p_send.at[target],
                recv_sem=p_recv.at[owner],
                device_id=(target, n),
                device_id_type=MESH,
            ),
        )

    @pl.loop(1, wide_count)
    def _(k):
        for copy in query_copies(w, lax.rem(w + k, wide_count)):
            copy.start()

    def encode(c, size):
        cols = pl.ds(pl.multiple_of(c * CHUNK, CHUNK), size)
        held = ROWS // seq
        for i in range(passages // held):
            x = x_ref[i * ROWS : (i + 1) * ROWS, :]
            gate = jnp.dot(x, gate_v[:, cols], preferred_element_type=jnp.float32)
            upward = jnp.dot(x, up_v[:, cols], preferred_element_type=jnp.float32)
            hidden = gate * upward * (1.0 + jnp.tanh(0.5 * gate))
            summed = jnp.sum(hidden.reshape(held, seq, size), axis=1)
            hidden_sum[c, i * held : (i + 1) * held, :size] = summed * (0.5 / seq)

    def project(c, size):
        mean = hidden_sum[c, :, :size]
        high = mean.astype(jnp.bfloat16)
        low = (mean - high.astype(jnp.float32)).astype(jnp.bfloat16)
        rows = pl.ds(pl.multiple_of(c * CHUNK, CHUNK), size)
        total[...] += jnp.dot(
            jnp.concatenate([high, low], axis=0),
            down_v[rows, :],
            preferred_element_type=jnp.float32,
        )

    total[...] = jnp.zeros_like(total)

    @pl.loop(0, LOADS)
    def _(c):
        for copy in weight_copies(c):
            copy.wait()

    encode(0, CHUNK)
    down_copy.wait()

    @pl.loop(1, full)
    def _(c):
        project(c - 1, CHUNK)
        encode(c, CHUNK)

    project(full - 1, CHUNK)
    if tail:
        encode(full, tail)
        project(full, tail)

    branch = total[:passages, :] + total[passages:, :] + token_mean[...] * (1.0 / narrow_count)
    for j in range(narrow_count):
        for g in range(groups):
            part[j, g * per : (g + 1) * per, :] = branch[
                j * per : (j + 1) * per, g * lanes : (g + 1) * lanes
            ]

    def part_copy(sender, target):
        return pltpu.make_async_remote_copy(
            src_ref=part.at[target],
            dst_ref=part_in.at[sender],
            send_sem=part_send.at[target],
            recv_sem=part_recv.at[sender],
            device_id=(w, target),
            device_id_type=MESH,
        )

    for k in range(1, narrow_count):
        part_copy(n, lax.rem(n + k, narrow_count)).start()

    own_q.wait()
    own_p.wait()

    @pl.loop(1, wide_count)
    def _(k):
        for copy in query_copies(lax.rem(w + k, wide_count), w):
            copy.wait_recv()

    lane = lax.broadcasted_iota(jnp.int32, (1, 128), 1)
    pieces = []
    for t in range(steps):
        blocks[t * block : (t + 1) * block, :] = q_all[owners_ref[t]]
    for t in range(0, steps, 2):
        pieces.append(
            jnp.where(
                lane < block,
                p_all[owners_ref[t]][0:1, :],
                p_all[owners_ref[t + 1]][0:1, :],
            )
        )
    chosen = jnp.concatenate(pieces, axis=1)
    factor = 1.0 / math.sqrt(width)
    contract = (((1,), (1,)), ((), ()))
    slab_copy.wait()
    old_rows = slab_ref.shape[0]
    tile = 512

    def old_tile(i, carry):
        top, mass, picked = carry
        rows = pl.ds(pl.multiple_of(i * tile, tile), tile)
        scores = factor * lax.dot_general(
            slab_v[rows, :], blocks[...], contract, preferred_element_type=jnp.float32
        )
        numbers = me * old_rows + i * tile + lax.broadcasted_iota(jnp.int32, (tile, 1), 0)
        picked += jnp.sum(jnp.where(numbers == chosen, scores, 0.0), axis=0, keepdims=True)
        new_top = jnp.maximum(top, jnp.max(scores, axis=0, keepdims=True))
        mass = mass * jnp.exp(top - new_top) + jnp.sum(
            jnp.exp(scores - new_top), axis=0, keepdims=True
        )
        return new_top, mass, picked

    zero = jnp.zeros((1, count), jnp.float32)
    top, mass, picked = lax.fori_loop(
        0, old_rows // tile, old_tile, (jnp.full((1, count), -jnp.inf, jnp.float32), zero, zero)
    )

    pooled = part[n]
    for k in range(1, narrow_count):
        other = lax.rem(n + k, narrow_count)
        part_copy(other, n).wait_recv()
        pooled += part_in[other]
    square = jnp.sum(pooled * pooled, axis=1, keepdims=True)
    square = sum(square[g * per : (g + 1) * per] for g in range(groups)) * (1.0 / width)
    norm = lax.rsqrt(jnp.concatenate([square] * groups, axis=0) + EPS)
    folded = (pooled * norm * out_gain_ref[...]).astype(jnp.bfloat16).astype(jnp.float32)
    rows = jnp.concatenate([folded[g * per : (g + 1) * per] for g in range(groups)], axis=1)
    rows = jnp.concatenate([rows, jnp.zeros((MSG - per, width), jnp.float32)], axis=0)

    piece = width // SPLIT
    spread = jnp.concatenate([rows[:8, j * piece : (j + 1) * piece] for j in range(SPLIT)], axis=0)
    outgoing = jnp.dot(place_ref[...], spread.astype(jnp.bfloat16), preferred_element_type=jnp.float32)
    messages[...] = outgoing.astype(jnp.bfloat16).reshape(wide_count, MSG, piece)
    holder = w // sources
    slot = lax.rem(w, sources) * narrow_count + n

    def message_copy(target, at):
        return pltpu.make_async_remote_copy(
            src_ref=messages.at[target],
            dst_ref=messages_in.at[at],
            send_sem=msg_send.at[target],
            recv_sem=msg_recv.at[at],
            device_id=(target, holder),
            device_id_type=MESH,
        )

    local_message = pltpu.make_async_copy(
        messages.at[w], messages_in.at[slot], own_sem.at[2]
    )

    @pl.loop(1, wide_count)
    def _(k):
        message_copy(lax.rem(w + k, wide_count), slot).start()

    @pl.when(holder == n)
    def _():
        local_message.start()

    @pl.when(holder != n)
    def _():
        message_copy(w, slot).start()

    scores = factor * lax.dot_general(
        rows.astype(jnp.bfloat16), blocks[...], contract, preferred_element_type=jnp.float32
    )
    place = lax.broadcasted_iota(jnp.int32, (MSG, 1), 0)
    valid = place < per
    numbers = devices * old_rows + w * passages + n * per + place
    picked += jnp.sum(jnp.where(valid & (numbers == chosen), scores, 0.0), axis=0, keepdims=True)
    masked = jnp.where(valid, scores, -jnp.inf)
    new_top = jnp.maximum(top, jnp.max(masked, axis=0, keepdims=True))
    mass = mass * jnp.exp(top - new_top) + jnp.sum(
        jnp.exp(masked - new_top), axis=0, keepdims=True
    )
    halves = count // 128
    stat = [v[:, h * 128 : (h + 1) * 128] for v in (new_top, mass, picked) for h in range(halves)]
    stat.append(jnp.zeros((8 - 3 * halves, 128), jnp.float32))
    stats[me] = jnp.concatenate(stat, axis=0)

    def stat_copy(sender, target):
        return pltpu.make_async_remote_copy(
            src_ref=stats.at[sender],
            dst_ref=stats.at[sender],
            send_sem=stat_send.at[target],
            recv_sem=stat_recv.at[sender],
            device_id=(target // narrow_count, lax.rem(target, narrow_count)),
            device_id_type=MESH,
        )

    @pl.loop(1, devices)
    def _(k):
        stat_copy(me, lax.rem(me + k, devices)).start()

    @pl.loop(0, sources)
    def _(a):
        @pl.loop(0, narrow_count)
        def _(b):
            at = a * narrow_count + b

            @pl.when((n * sources + a == w) & (b == n))
            def _():
                local_message.wait()

            @pl.when((n * sources + a != w) | (b != n))
            def _():
                message_copy(w, at).wait_recv()

    for a in range(sources):
        held = messages_in[a * narrow_count].astype(jnp.float32)
        for b in range(1, narrow_count):
            held += messages_in[a * narrow_count + b].astype(jnp.float32)
        index_ref[a] = held.astype(jnp.bfloat16)

    @pl.loop(1, devices)
    def _(k):
        stat_copy(lax.rem(me + k, devices), me).wait_recv()

    every = stats[...]
    tops = every[:, :halves, :]
    largest = jnp.max(tops, axis=0)
    masses = jnp.sum(every[:, halves : 2 * halves, :] * jnp.exp(tops - largest[None]), axis=0)
    chosen_score = jnp.sum(every[:, 2 * halves : 3 * halves, :], axis=0)
    losses_ref[...] = largest + jnp.log(masses) - chosen_score

    @pl.loop(1, wide_count)
    def _(k):
        target = lax.rem(w + k, wide_count)
        for copy in query_copies(w, target):
            copy.wait_send()
        message_copy(target, slot).wait_send()

    @pl.when(holder != n)
    def _():
        message_copy(w, slot).wait_send()

    for k in range(1, narrow_count):
        part_copy(n, lax.rem(n + k, narrow_count)).wait_send()

    @pl.loop(1, devices)
    def _(k):
        stat_copy(me, lax.rem(me + k, devices)).wait_send()


def local(
    tokens,
    ln_gain,
    gate_weight,
    up_weight,
    down_weight,
    out_gain,
    shard_ids,
    slab_old,
    queries,
    positives,
    owners,
):
    passages, seq, width = tokens.shape
    narrow_count = lax.axis_size("narrow")
    wide_count = lax.axis_size("wide")
    narrow_rank = lax.axis_index("narrow")
    units = gate_weight.shape[1]
    steps, block = owners.shape[0], queries.shape[1]
    count = steps * block
    per = passages // narrow_count
    capacity = 2 * passages // wide_count
    sources = wide_count // narrow_count
    devices = wide_count * narrow_count
    groups = 8 // per
    lanes = width // groups
    piece = width // SPLIT
    chunks = -(-units // CHUNK)

    positions = jnp.arange(passages, dtype=jnp.int32)
    earlier = positions[:, None] > positions[None, :]
    same = shard_ids[:, None] == shard_ids[None, :]
    rank = jnp.sum((earlier & same).astype(jnp.int32), axis=1)
    slots = shard_ids * capacity + rank
    own = lax.dynamic_slice_in_dim(slots, narrow_rank * per, per, 0)
    own = jnp.concatenate([own, jnp.full((8 - per,), -1, jnp.int32)])
    row = jnp.arange(wide_count * MSG, dtype=jnp.int32)[:, None]
    shard, inner = row // MSG, row % MSG
    column = jnp.arange(SPLIT * 8, dtype=jnp.int32)[None, :]
    place = (
        (inner < SPLIT * capacity)
        & (inner // capacity == column // 8)
        & (jnp.tile(own, SPLIT)[None, :] == shard * capacity + inner % capacity)
    ).astype(jnp.bfloat16)

    gain_out = jnp.repeat(out_gain.astype(jnp.float32).reshape(groups, lanes), per, axis=0)
    paired = jnp.broadcast_to(jnp.concatenate([positives, positives], axis=1), (8, 2 * block))

    vmem = pl.BlockSpec(memory_space=pltpu.VMEM)
    anywhere = pl.BlockSpec(memory_space=pl.ANY)
    dma = pltpu.SemaphoreType.DMA
    flops = 4 * passages * seq * width * units + 2 * count * width * slab_old.shape[0]
    moved = 2 * width * (passages * seq + 3 * units + slab_old.shape[0])
    index_part, losses = pl.pallas_call(
        functools.partial(kernel, (passages, seq, wide_count, narrow_count, steps, block)),
        out_shape=(
            jax.ShapeDtypeStruct((sources, MSG, piece), jnp.bfloat16),
            jax.ShapeDtypeStruct((count // 128, 128), jnp.float32),
        ),
        in_specs=[
            anywhere,
            vmem,
            anywhere,
            anywhere,
            anywhere,
            vmem,
            vmem,
            anywhere,
            anywhere,
            vmem,
            pl.BlockSpec(memory_space=pltpu.SMEM),
        ],
        out_specs=(vmem, vmem),
        scratch_shapes=[
            pltpu.VMEM((passages * seq, width), jnp.bfloat16),
            pltpu.VMEM((width, units), jnp.bfloat16),
            pltpu.VMEM((width, units), jnp.bfloat16),
            pltpu.VMEM((units, width), jnp.bfloat16),
            pltpu.VMEM(slab_old.shape, jnp.bfloat16),
            pltpu.VMEM((wide_count, block, width), jnp.bfloat16),
            pltpu.VMEM((wide_count, 8, 2 * block), jnp.int32),
            pltpu.VMEM((count, width), jnp.bfloat16),
            pltpu.VMEM((chunks, passages, CHUNK), jnp.float32),
            pltpu.VMEM((passages, width), jnp.float32),
            pltpu.VMEM((2 * passages, width), jnp.float32),
            pltpu.VMEM((narrow_count, 8, lanes), jnp.float32),
            pltpu.VMEM((narrow_count, 8, lanes), jnp.float32),
            pltpu.VMEM((wide_count, MSG, piece), jnp.bfloat16),
            pltpu.VMEM((sources * narrow_count, MSG, piece), jnp.bfloat16),
            pltpu.VMEM((devices, 8, 128), jnp.float32),
            dma((passages,)),
            dma((2, LOADS)),
            dma((2,)),
            dma((3,)),
            dma((wide_count,)),
            dma((wide_count,)),
            dma((wide_count,)),
            dma((wide_count,)),
            dma((narrow_count,)),
            dma((narrow_count,)),
            dma((wide_count,)),
            dma((sources * narrow_count,)),
            dma((devices,)),
            dma((devices,)),
        ],
        compiler_params=pltpu.CompilerParams(
            collective_id=0, has_side_effects=True, vmem_limit_bytes=58 * 1024 * 1024
        ),
        cost_estimate=pl.CostEstimate(
            flops=flops, bytes_accessed=moved, transcendentals=passages * seq * units
        ),
    )(
        tokens.reshape(passages * seq, width),
        ln_gain.astype(jnp.float32).reshape(1, width),
        gate_weight,
        up_weight,
        down_weight,
        gain_out,
        place,
        slab_old,
        queries[0],
        paired,
        owners,
    )
    arrived = index_part[:, : SPLIT * capacity].reshape(sources, SPLIT, capacity, piece)
    arrived = arrived.transpose(0, 2, 1, 3).reshape(1, sources, capacity, width)
    return arrived, losses.reshape(steps, block)


def solution(mesh):
    return jax.shard_map(
        local,
        mesh=mesh,
        in_specs=(
            P("wide", None, None),
            P(),
            P(None, "narrow"),
            P(None, "narrow"),
            P("narrow", None),
            P(),
            P("wide"),
            P(("wide", "narrow"), None),
            P("wide", None, None),
            P("wide", None),
            P(),
        ),
        out_specs=(P("wide", "narrow", None, None), P()),
        check_vma=False,
    )
```

```python
import functools
import math

import jax
import jax.numpy as jnp
from jax import lax
from jax.experimental import pallas as pl
from jax.experimental.pallas import tpu as pltpu
from jax.sharding import PartitionSpec as P

EPS = 1e-06
MESH = pl.DeviceIdType.MESH
CHUNK = 256
ROWS = 512
SPLIT = 4
MSG = 16


def kernel(
    dims,
    tokens_ref,
    gains_ref,
    gate_ref,
    up_ref,
    down_ref,
    shards_ref,
    slab_ref,
    queries_ref,
    positives_ref,
    owners_ref,
    index_ref,
    losses_ref,
    x_ref,
    gate_v,
    up_v,
    down_v,
    slab_v,
    q_all,
    p_own,
    p_all,
    blocks,
    hidden_sum,
    token_mean,
    total,
    part,
    part_in,
    messages,
    messages_in,
    stats,
    x_sem,
    w_sem,
    big_sem,
    own_sem,
    q_send,
    q_recv,
    p_send,
    p_recv,
    part_send,
    part_recv,
    msg_send,
    msg_recv,
    stat_send,
    stat_recv,
):
    passages, seq, wide_count, narrow_count, steps, block = dims
    width = tokens_ref.shape[1]
    units = gate_ref.shape[0]
    capacity = index_ref.shape[1]
    full, tail = units // CHUNK, units % CHUNK
    per = passages // narrow_count
    groups = 8 // per
    lanes = width // groups
    sources = wide_count // narrow_count
    devices = wide_count * narrow_count
    count = steps * block
    w = lax.axis_index("wide")
    n = lax.axis_index("narrow")
    me = w * narrow_count + n

    def token_copy(i):
        rows = pl.ds(pl.multiple_of(i * seq, seq), seq)
        return pltpu.make_async_copy(tokens_ref.at[rows, :], x_ref.at[rows, :], x_sem.at[i])

    def weight_copies(c, size):
        rows = pl.ds(pl.multiple_of(c * CHUNK, CHUNK), size)
        return (
            pltpu.make_async_copy(gate_ref.at[rows, :], gate_v.at[rows, :], w_sem.at[0, c]),
            pltpu.make_async_copy(up_ref.at[rows, :], up_v.at[rows, :], w_sem.at[1, c]),
        )

    down_copy = pltpu.make_async_copy(down_ref, down_v, big_sem.at[0])
    slab_copy = pltpu.make_async_copy(slab_ref, slab_v, big_sem.at[1])
    own_q = pltpu.make_async_copy(queries_ref, q_all.at[w], own_sem.at[0])

    @pl.loop(0, passages)
    def _(i):
        token_copy(i).start()

    @pl.loop(0, full)
    def _(c):
        for copy in weight_copies(c, CHUNK):
            copy.start()

    if tail:
        for copy in weight_copies(full, tail):
            copy.start()
    down_copy.start()
    slab_copy.start()
    own_q.start()

    barrier = pltpu.get_barrier_semaphore()

    @pl.loop(1, devices)
    def _(k):
        other = lax.rem(me + k, devices)
        pl.semaphore_signal(
            barrier,
            inc=1,
            device_id=(other // narrow_count, lax.rem(other, narrow_count)),
            device_id_type=MESH,
        )

    gain = gains_ref[0:1, :]
    p_own[...] = jnp.zeros_like(p_own)
    p_own[0:1, :block] = positives_ref[...]
    p_own[0:1, block:] = positives_ref[...]
    p_all[w] = p_own[...]

    @pl.loop(0, passages)
    def _(i):
        token_copy(i).wait()
        rows = pl.ds(pl.multiple_of(i * seq, seq), seq)
        values = x_ref[rows, :].astype(jnp.float32)
        scale = lax.rsqrt(jnp.mean(values * values, axis=1, keepdims=True) + EPS)
        token_mean[pl.ds(i, 1), :] = jnp.sum(values, axis=0, keepdims=True) * (1.0 / seq)
        x_ref[rows, :] = (values * scale * gain).astype(jnp.bfloat16)

    pl.semaphore_wait(barrier, devices - 1)

    def query_copies(owner, target):
        return (
            pltpu.make_async_remote_copy(
                src_ref=queries_ref,
                dst_ref=q_all.at[owner],
                send_sem=q_send.at[target],
                recv_sem=q_recv.at[owner],
                device_id=(target, n),
                device_id_type=MESH,
            ),
            pltpu.make_async_remote_copy(
                src_ref=p_own,
                dst_ref=p_all.at[owner],
                send_sem=p_send.at[target],
                recv_sem=p_recv.at[owner],
                device_id=(target, n),
                device_id_type=MESH,
            ),
        )

    @pl.loop(1, wide_count)
    def _(k):
        for copy in query_copies(w, lax.rem(w + k, wide_count)):
            copy.start()

    contract = (((1,), (1,)), ((), ()))

    def encode(c, size):
        units_of = pl.ds(pl.multiple_of(c * CHUNK, CHUNK), size)
        held = ROWS // seq
        for i in range(passages // held):
            x = x_ref[i * ROWS : (i + 1) * ROWS, :]
            gate = lax.dot_general(x, gate_v[units_of, :], contract, preferred_element_type=jnp.float32)
            upward = lax.dot_general(x, up_v[units_of, :], contract, preferred_element_type=jnp.float32)
            hidden = gate * upward * (1.0 + jnp.tanh(0.5 * gate))
            summed = jnp.sum(hidden.reshape(held, seq, size), axis=1)
            hidden_sum[c, i * held : (i + 1) * held, :size] = summed * (0.5 / seq)

    def project(c, size):
        mean = hidden_sum[c, :, :size]
        high = mean.astype(jnp.bfloat16)
        low = (mean - high.astype(jnp.float32)).astype(jnp.bfloat16)
        rows = pl.ds(pl.multiple_of(c * CHUNK, CHUNK), size)
        total[...] += jnp.dot(
            jnp.concatenate([high, low], axis=0),
            down_v[rows, :],
            preferred_element_type=jnp.float32,
        )

    total[...] = jnp.zeros_like(total)

    for copy in weight_copies(0, CHUNK):
        copy.wait()
    encode(0, CHUNK)
    down_copy.wait()

    @pl.loop(1, full)
    def _(c):
        for copy in weight_copies(c, CHUNK):
            copy.wait()
        project(c - 1, CHUNK)
        encode(c, CHUNK)

    project(full - 1, CHUNK)
    if tail:
        for copy in weight_copies(full, tail):
            copy.wait()
        encode(full, tail)
        project(full, tail)

    branch = total[:passages, :] + total[passages:, :] + token_mean[...] * (1.0 / narrow_count)
    for j in range(narrow_count):
        for g in range(groups):
            part[j, g * per : (g + 1) * per, :] = branch[
                j * per : (j + 1) * per, g * lanes : (g + 1) * lanes
            ]

    def part_copy(sender, target):
        return pltpu.make_async_remote_copy(
            src_ref=part.at[target],
            dst_ref=part_in.at[sender],
            send_sem=part_send.at[target],
            recv_sem=part_recv.at[sender],
            device_id=(w, target),
            device_id_type=MESH,
        )

    for k in range(1, narrow_count):
        part_copy(n, lax.rem(n + k, narrow_count)).start()

    own_q.wait()

    @pl.loop(1, wide_count)
    def _(k):
        for copy in query_copies(lax.rem(w + k, wide_count), w):
            copy.wait_recv()

    lane = lax.broadcasted_iota(jnp.int32, (1, 128), 1)
    pieces = []
    for t in range(steps):
        blocks[t * block : (t + 1) * block, :] = q_all[owners_ref[t]]
    for t in range(0, steps, 2):
        pieces.append(
            jnp.where(
                lane < block,
                p_all[owners_ref[t]][0:1, :],
                p_all[owners_ref[t + 1]][0:1, :],
            )
        )
    chosen = jnp.concatenate(pieces, axis=1)
    factor = 1.0 / math.sqrt(width)
    slab_copy.wait()
    old_rows = slab_ref.shape[0]
    tile = 512

    def old_tile(i, carry):
        top, mass, picked = carry
        rows = pl.ds(pl.multiple_of(i * tile, tile), tile)
        scores = factor * lax.dot_general(
            slab_v[rows, :], blocks[...], contract, preferred_element_type=jnp.float32
        )
        numbers = me * old_rows + i * tile + lax.broadcasted_iota(jnp.int32, (tile, 1), 0)
        picked += jnp.sum(jnp.where(numbers == chosen, scores, 0.0), axis=0, keepdims=True)
        new_top = jnp.maximum(top, jnp.max(scores, axis=0, keepdims=True))
        mass = mass * jnp.exp(top - new_top) + jnp.sum(
            jnp.exp(scores - new_top), axis=0, keepdims=True
        )
        return new_top, mass, picked

    zero = jnp.zeros((1, count), jnp.float32)
    top, mass, picked = lax.fori_loop(
        0, old_rows // tile, old_tile, (jnp.full((1, count), -jnp.inf, jnp.float32), zero, zero)
    )

    row = lax.broadcasted_iota(jnp.int32, (wide_count * MSG, SPLIT * 8), 0)
    column = lax.broadcasted_iota(jnp.int32, (wide_count * MSG, SPLIT * 8), 1)
    inner = row % MSG
    wanted = (row // MSG) * capacity + inner % capacity
    lined = (inner < SPLIT * capacity) & (inner // capacity == column // 8)
    place = jnp.zeros((wide_count * MSG, SPLIT * 8), jnp.float32)
    for p in range(per):
        at = n * per + p
        shard = shards_ref[at]
        rank = 0
        for q in range(passages):
            rank += jnp.where((q < at) & (shards_ref[q] == shard), 1, 0)
        hit = lined & (column % 8 == p) & (wanted == shard * capacity + rank)
        place = jnp.where(hit, 1.0, place)
    place = place.astype(jnp.bfloat16)

    pooled = part[n]
    for k in range(1, narrow_count):
        other = lax.rem(n + k, narrow_count)
        part_copy(other, n).wait_recv()
        pooled += part_in[other]
    gain_out = jnp.concatenate(
        [
            jnp.broadcast_to(gains_ref[1:2, g * lanes : (g + 1) * lanes], (per, lanes))
            for g in range(groups)
        ],
        axis=0,
    )
    square = jnp.sum(pooled * pooled, axis=1, keepdims=True)
    square = sum(square[g * per : (g + 1) * per] for g in range(groups)) * (1.0 / width)
    norm = lax.rsqrt(jnp.concatenate([square] * groups, axis=0) + EPS)
    folded = (pooled * norm * gain_out).astype(jnp.bfloat16).astype(jnp.float32)
    rows = jnp.concatenate([folded[g * per : (g + 1) * per] for g in range(groups)], axis=1)
    rows = jnp.concatenate([rows, jnp.zeros((MSG - per, width), jnp.float32)], axis=0)

    piece = width // SPLIT
    spread = jnp.concatenate([rows[:8, j * piece : (j + 1) * piece] for j in range(SPLIT)], axis=0)
    outgoing = jnp.dot(place, spread.astype(jnp.bfloat16), preferred_element_type=jnp.float32)
    messages[...] = outgoing.astype(jnp.bfloat16).reshape(wide_count, MSG, piece)
    holder = w // sources
    slot = lax.rem(w, sources) * narrow_count + n

    def message_copy(target, at):
        return pltpu.make_async_remote_copy(
            src_ref=messages.at[target],
            dst_ref=messages_in.at[at],
            send_sem=msg_send.at[target],
            recv_sem=msg_recv.at[at],
            device_id=(target, holder),
            device_id_type=MESH,
        )

    local_message = pltpu.make_async_copy(
        messages.at[w], messages_in.at[slot], own_sem.at[2]
    )

    @pl.loop(1, wide_count)
    def _(k):
        message_copy(lax.rem(w + k, wide_count), slot).start()

    @pl.when(holder == n)
    def _():
        local_message.start()

    @pl.when(holder != n)
    def _():
        message_copy(w, slot).start()

    scores = factor * lax.dot_general(
        rows.astype(jnp.bfloat16), blocks[...], contract, preferred_element_type=jnp.float32
    )
    spot = lax.broadcasted_iota(jnp.int32, (MSG, 1), 0)
    valid = spot < per
    numbers = devices * old_rows + w * passages + n * per + spot
    picked += jnp.sum(jnp.where(valid & (numbers == chosen), scores, 0.0), axis=0, keepdims=True)
    masked = jnp.where(valid, scores, -jnp.inf)
    new_top = jnp.maximum(top, jnp.max(masked, axis=0, keepdims=True))
    mass = mass * jnp.exp(top - new_top) + jnp.sum(
        jnp.exp(masked - new_top), axis=0, keepdims=True
    )
    halves = count // 128
    stat = [v[:, h * 128 : (h + 1) * 128] for v in (new_top, mass, picked) for h in range(halves)]
    stat.append(jnp.zeros((8 - 3 * halves, 128), jnp.float32))
    stats[me] = jnp.concatenate(stat, axis=0)

    def stat_copy(sender, target):
        return pltpu.make_async_remote_copy(
            src_ref=stats.at[sender],
            dst_ref=stats.at[sender],
            send_sem=stat_send.at[target],
            recv_sem=stat_recv.at[sender],
            device_id=(target // narrow_count, lax.rem(target, narrow_count)),
            device_id_type=MESH,
        )

    @pl.loop(1, devices)
    def _(k):
        stat_copy(me, lax.rem(me + k, devices)).start()

    @pl.loop(0, sources)
    def _(a):
        @pl.loop(0, narrow_count)
        def _(b):
            at = a * narrow_count + b

            @pl.when((n * sources + a == w) & (b == n))
            def _():
                local_message.wait()

            @pl.when((n * sources + a != w) | (b != n))
            def _():
                message_copy(w, at).wait_recv()

    for a in range(sources):
        held = messages_in[a * narrow_count].astype(jnp.float32)
        for b in range(1, narrow_count):
            held += messages_in[a * narrow_count + b].astype(jnp.float32)
        index_ref[a] = jnp.concatenate(
            [held[j * capacity : (j + 1) * capacity] for j in range(SPLIT)], axis=1
        ).astype(jnp.bfloat16)

    @pl.loop(1, devices)
    def _(k):
        stat_copy(lax.rem(me + k, devices), me).wait_recv()

    every = stats[...]
    tops = every[:, :halves, :]
    largest = jnp.max(tops, axis=0)
    masses = jnp.sum(every[:, halves : 2 * halves, :] * jnp.exp(tops - largest[None]), axis=0)
    chosen_score = jnp.sum(every[:, 2 * halves : 3 * halves, :], axis=0)
    loss = largest + jnp.log(masses) - chosen_score
    for t in range(steps):
        side = t % 2 * block
        losses_ref[t : t + 1, :] = loss[t // 2 : t // 2 + 1, side : side + block]

    @pl.loop(1, wide_count)
    def _(k):
        target = lax.rem(w + k, wide_count)
        for copy in query_copies(w, target):
            copy.wait_send()
        message_copy(target, slot).wait_send()

    @pl.when(holder != n)
    def _():
        message_copy(w, slot).wait_send()

    for k in range(1, narrow_count):
        part_copy(n, lax.rem(n + k, narrow_count)).wait_send()

    @pl.loop(1, devices)
    def _(k):
        stat_copy(me, lax.rem(me + k, devices)).wait_send()


def local(
    tokens,
    ln_gain,
    gate_weight,
    up_weight,
    down_weight,
    out_gain,
    shard_ids,
    slab_old,
    queries,
    positives,
    owners,
):
    passages, seq, width = tokens.shape
    narrow_count = lax.axis_size("narrow")
    wide_count = lax.axis_size("wide")
    units = gate_weight.shape[1]
    steps, block = owners.shape[0], queries.shape[1]
    count = steps * block
    per = passages // narrow_count
    capacity = 2 * passages // wide_count
    sources = wide_count // narrow_count
    devices = wide_count * narrow_count
    groups = 8 // per
    lanes = width // groups
    piece = width // SPLIT
    chunks = -(-units // CHUNK)

    gains = jnp.stack([ln_gain, out_gain]).astype(jnp.float32)
    vmem = pl.BlockSpec(memory_space=pltpu.VMEM)
    anywhere = pl.BlockSpec(memory_space=pl.ANY)
    smem = pl.BlockSpec(memory_space=pltpu.SMEM)
    dma = pltpu.SemaphoreType.DMA
    flops = 4 * passages * seq * width * units + 2 * count * width * slab_old.shape[0]
    moved = 2 * width * (passages * seq + 3 * units + slab_old.shape[0])
    index_part, losses = pl.pallas_call(
        functools.partial(kernel, (passages, seq, wide_count, narrow_count, steps, block)),
        out_shape=(
            jax.ShapeDtypeStruct((sources, capacity, width), jnp.bfloat16),
            jax.ShapeDtypeStruct((steps, block), jnp.float32),
        ),
        in_specs=[
            anywhere,
            vmem,
            anywhere,
            anywhere,
            anywhere,
            smem,
            anywhere,
            anywhere,
            vmem,
            smem,
        ],
        out_specs=(vmem, vmem),
        scratch_shapes=[
            pltpu.VMEM((passages * seq, width), jnp.bfloat16),
            pltpu.VMEM((units, width), jnp.bfloat16),
            pltpu.VMEM((units, width), jnp.bfloat16),
            pltpu.VMEM((units, width), jnp.bfloat16),
            pltpu.VMEM(slab_old.shape, jnp.bfloat16),
            pltpu.VMEM((wide_count, block, width), jnp.bfloat16),
            pltpu.VMEM((8, 2 * block), jnp.int32),
            pltpu.VMEM((wide_count, 8, 2 * block), jnp.int32),
            pltpu.VMEM((count, width), jnp.bfloat16),
            pltpu.VMEM((chunks, passages, CHUNK), jnp.float32),
            pltpu.VMEM((passages, width), jnp.float32),
            pltpu.VMEM((2 * passages, width), jnp.float32),
            pltpu.VMEM((narrow_count, 8, lanes), jnp.float32),
            pltpu.VMEM((narrow_count, 8, lanes), jnp.float32),
            pltpu.VMEM((wide_count, MSG, piece), jnp.bfloat16),
            pltpu.VMEM((sources * narrow_count, MSG, piece), jnp.bfloat16),
            pltpu.VMEM((devices, 8, 128), jnp.float32),
            dma((passages,)),
            dma((2, chunks)),
            dma((2,)),
            dma((3,)),
            dma((wide_count,)),
            dma((wide_count,)),
            dma((wide_count,)),
            dma((wide_count,)),
            dma((narrow_count,)),
            dma((narrow_count,)),
            dma((wide_count,)),
            dma((sources * narrow_count,)),
            dma((devices,)),
            dma((devices,)),
        ],
        compiler_params=pltpu.CompilerParams(
            collective_id=0, has_side_effects=True, vmem_limit_bytes=58 * 1024 * 1024
        ),
        cost_estimate=pl.CostEstimate(
            flops=flops, bytes_accessed=moved, transcendentals=passages * seq * units
        ),
    )(
        tokens.reshape(passages * seq, width),
        gains,
        gate_weight.T,
        up_weight.T,
        down_weight,
        shard_ids,
        slab_old,
        queries[0],
        positives,
        owners,
    )
    return index_part[None], losses


def solution(mesh):
    return jax.shard_map(
        local,
        mesh=mesh,
        in_specs=(
            P("wide", None, None),
            P(),
            P(None, "narrow"),
            P(None, "narrow"),
            P("narrow", None),
            P(),
            P("wide"),
            P(("wide", "narrow"), None),
            P("wide", None, None),
            P("wide", None),
            P(),
        ),
        out_specs=(P("wide", "narrow", None, None), P()),
        check_vma=False,
    )
```

```python
import functools
import math

import jax
import jax.numpy as jnp
from jax import lax
from jax.experimental import pallas as pl
from jax.experimental.pallas import tpu as pltpu
from jax.sharding import PartitionSpec as P

EPS = 1e-06
MESH = pl.DeviceIdType.MESH
CHUNK = 256
ROWS = 512
SPLIT = 4
MSG = 16


def kernel(
    dims,
    tokens_ref,
    ln_gain_ref,
    out_gain_ref,
    gate_ref,
    up_ref,
    down_ref,
    shards_ref,
    slab_ref,
    queries_ref,
    positives_ref,
    owners_ref,
    index_ref,
    losses_ref,
    x_ref,
    gate_v,
    up_v,
    down_v,
    slab_v,
    q_all,
    p_own,
    p_all,
    blocks,
    hidden_sum,
    token_mean,
    total,
    part,
    part_in,
    messages,
    messages_in,
    stats,
    x_sem,
    w_sem,
    big_sem,
    own_sem,
    q_send,
    q_recv,
    p_send,
    p_recv,
    part_send,
    part_recv,
    msg_send,
    msg_recv,
    stat_send,
    stat_recv,
):
    passages, seq, wide_count, narrow_count, steps, block = dims
    width = tokens_ref.shape[1]
    units = gate_ref.shape[0]
    capacity = index_ref.shape[1]
    full, tail = units // CHUNK, units % CHUNK
    per = passages // narrow_count
    groups = 8 // per
    lanes = width // groups
    sources = wide_count // narrow_count
    devices = wide_count * narrow_count
    count = steps * block
    w = lax.axis_index("wide")
    n = lax.axis_index("narrow")
    me = w * narrow_count + n

    def token_copy(i):
        rows = pl.ds(pl.multiple_of(i * seq, seq), seq)
        return pltpu.make_async_copy(tokens_ref.at[rows, :], x_ref.at[rows, :], x_sem.at[i])

    def weight_copies(c, size):
        rows = pl.ds(pl.multiple_of(c * CHUNK, CHUNK), size)
        return (
            pltpu.make_async_copy(gate_ref.at[rows, :], gate_v.at[rows, :], w_sem.at[0, c]),
            pltpu.make_async_copy(up_ref.at[rows, :], up_v.at[rows, :], w_sem.at[1, c]),
        )

    down_copy = pltpu.make_async_copy(down_ref, down_v, big_sem.at[0])
    slab_copy = pltpu.make_async_copy(slab_ref, slab_v, big_sem.at[1])
    own_q = pltpu.make_async_copy(queries_ref, q_all.at[w], own_sem.at[0])

    @pl.loop(0, passages)
    def _(i):
        token_copy(i).start()

    @pl.loop(0, full)
    def _(c):
        for copy in weight_copies(c, CHUNK):
            copy.start()

    if tail:
        for copy in weight_copies(full, tail):
            copy.start()
    down_copy.start()
    slab_copy.start()
    own_q.start()

    barrier = pltpu.get_barrier_semaphore()

    @pl.loop(1, devices)
    def _(k):
        other = lax.rem(me + k, devices)
        pl.semaphore_signal(
            barrier,
            inc=1,
            device_id=(other // narrow_count, lax.rem(other, narrow_count)),
            device_id_type=MESH,
        )

    gain = ln_gain_ref[...].astype(jnp.float32).reshape(1, width)
    p_own[...] = jnp.zeros_like(p_own)
    p_own[0:1, :block] = positives_ref[...]
    p_own[0:1, block:] = positives_ref[...]
    p_all[w] = p_own[...]

    held = ROWS // seq

    def normalize(i):
        for p in range(i * held, (i + 1) * held):
            token_copy(p).wait()
        for p in range(i * held, (i + 1) * held):
            rows = slice(p * seq, (p + 1) * seq)
            values = x_ref[rows, :].astype(jnp.float32)
            scale = lax.rsqrt(jnp.mean(values * values, axis=1, keepdims=True) + EPS)
            token_mean[p : p + 1, :] = jnp.sum(values, axis=0, keepdims=True) * (1.0 / seq)
            x_ref[rows, :] = (values * scale * gain).astype(jnp.bfloat16)

    normalize(0)
    pl.semaphore_wait(barrier, devices - 1)

    def query_copies(owner, target):
        return (
            pltpu.make_async_remote_copy(
                src_ref=queries_ref,
                dst_ref=q_all.at[owner],
                send_sem=q_send.at[target],
                recv_sem=q_recv.at[owner],
                device_id=(target, n),
                device_id_type=MESH,
            ),
            pltpu.make_async_remote_copy(
                src_ref=p_own,
                dst_ref=p_all.at[owner],
                send_sem=p_send.at[target],
                recv_sem=p_recv.at[owner],
                device_id=(target, n),
                device_id_type=MESH,
            ),
        )

    @pl.loop(1, wide_count)
    def _(k):
        for copy in query_copies(w, lax.rem(w + k, wide_count)):
            copy.start()

    contract = (((1,), (1,)), ((), ()))

    def encode(c, size, first=False):
        units_of = pl.ds(pl.multiple_of(c * CHUNK, CHUNK), size)
        for i in range(passages // held):
            if first and i + 1 < passages // held:
                normalize(i + 1)
            x = x_ref[i * ROWS : (i + 1) * ROWS, :]
            gate = lax.dot_general(x, gate_v[units_of, :], contract, preferred_element_type=jnp.float32)
            upward = lax.dot_general(x, up_v[units_of, :], contract, preferred_element_type=jnp.float32)
            hidden = gate * upward * (1.0 + jnp.tanh(0.5 * gate))
            summed = jnp.sum(hidden.reshape(held, seq, size), axis=1)
            hidden_sum[c, i * held : (i + 1) * held, :size] = summed * (0.5 / seq)

    def project(c, size):
        mean = hidden_sum[c, :, :size]
        high = mean.astype(jnp.bfloat16)
        low = (mean - high.astype(jnp.float32)).astype(jnp.bfloat16)
        rows = pl.ds(pl.multiple_of(c * CHUNK, CHUNK), size)
        total[...] += jnp.dot(
            jnp.concatenate([high, low], axis=0),
            down_v[rows, :],
            preferred_element_type=jnp.float32,
        )

    total[...] = jnp.zeros_like(total)

    for copy in weight_copies(0, CHUNK):
        copy.wait()
    encode(0, CHUNK, True)
    down_copy.wait()

    @pl.loop(1, full)
    def _(c):
        for copy in weight_copies(c, CHUNK):
            copy.wait()
        project(c - 1, CHUNK)
        encode(c, CHUNK)

    project(full - 1, CHUNK)
    if tail:
        for copy in weight_copies(full, tail):
            copy.wait()
        encode(full, tail)
        project(full, tail)

    branch = total[:passages, :] + total[passages:, :] + token_mean[...] * (1.0 / narrow_count)
    for j in range(narrow_count):
        for g in range(groups):
            part[j, g * per : (g + 1) * per, :] = branch[
                j * per : (j + 1) * per, g * lanes : (g + 1) * lanes
            ]

    def part_copy(sender, target):
        return pltpu.make_async_remote_copy(
            src_ref=part.at[target],
            dst_ref=part_in.at[sender],
            send_sem=part_send.at[target],
            recv_sem=part_recv.at[sender],
            device_id=(w, target),
            device_id_type=MESH,
        )

    for k in range(1, narrow_count):
        part_copy(n, lax.rem(n + k, narrow_count)).start()

    own_q.wait()

    @pl.loop(1, wide_count)
    def _(k):
        for copy in query_copies(lax.rem(w + k, wide_count), w):
            copy.wait_recv()

    lane = lax.broadcasted_iota(jnp.int32, (1, 128), 1)
    pieces = []
    for t in range(steps):
        blocks[t * block : (t + 1) * block, :] = q_all[owners_ref[t]]
    for t in range(0, steps, 2):
        pieces.append(
            jnp.where(
                lane < block,
                p_all[owners_ref[t]][0:1, :],
                p_all[owners_ref[t + 1]][0:1, :],
            )
        )
    chosen = jnp.concatenate(pieces, axis=1)
    factor = 1.0 / math.sqrt(width)
    slab_copy.wait()
    old_rows = slab_ref.shape[0]
    tile = 512

    def old_tile(i, carry):
        top, mass, picked = carry
        rows = pl.ds(pl.multiple_of(i * tile, tile), tile)
        scores = factor * lax.dot_general(
            slab_v[rows, :], blocks[...], contract, preferred_element_type=jnp.float32
        )
        numbers = me * old_rows + i * tile + lax.broadcasted_iota(jnp.int32, (tile, 1), 0)
        picked += jnp.sum(jnp.where(numbers == chosen, scores, 0.0), axis=0, keepdims=True)
        new_top = jnp.maximum(top, jnp.max(scores, axis=0, keepdims=True))
        mass = mass * jnp.exp(top - new_top) + jnp.sum(
            jnp.exp(scores - new_top), axis=0, keepdims=True
        )
        return new_top, mass, picked

    zero = jnp.zeros((1, count), jnp.float32)
    top, mass, picked = lax.fori_loop(
        0, old_rows // tile, old_tile, (jnp.full((1, count), -jnp.inf, jnp.float32), zero, zero)
    )

    row = lax.broadcasted_iota(jnp.int32, (wide_count * MSG, SPLIT * 8), 0)
    column = lax.broadcasted_iota(jnp.int32, (wide_count * MSG, SPLIT * 8), 1)
    inner = row % MSG
    wanted = (row // MSG) * capacity + inner % capacity
    lined = (inner < SPLIT * capacity) & (inner // capacity == column // 8)
    place = jnp.zeros((wide_count * MSG, SPLIT * 8), jnp.float32)
    for p in range(per):
        at = n * per + p
        shard = shards_ref[at]
        rank = 0
        for q in range(passages):
            rank += jnp.where((q < at) & (shards_ref[q] == shard), 1, 0)
        hit = lined & (column % 8 == p) & (wanted == shard * capacity + rank)
        place = jnp.where(hit, 1.0, place)
    place = place.astype(jnp.bfloat16)

    pooled = part[n]
    for k in range(1, narrow_count):
        other = lax.rem(n + k, narrow_count)
        part_copy(other, n).wait_recv()
        pooled += part_in[other]
    gain_row = out_gain_ref[...].astype(jnp.float32).reshape(1, width)
    gain_out = jnp.concatenate(
        [
            jnp.broadcast_to(gain_row[:, g * lanes : (g + 1) * lanes], (per, lanes))
            for g in range(groups)
        ],
        axis=0,
    )
    square = jnp.sum(pooled * pooled, axis=1, keepdims=True)
    square = sum(square[g * per : (g + 1) * per] for g in range(groups)) * (1.0 / width)
    norm = lax.rsqrt(jnp.concatenate([square] * groups, axis=0) + EPS)
    folded = (pooled * norm * gain_out).astype(jnp.bfloat16).astype(jnp.float32)
    rows = jnp.concatenate([folded[g * per : (g + 1) * per] for g in range(groups)], axis=1)
    rows = jnp.concatenate([rows, jnp.zeros((MSG - per, width), jnp.float32)], axis=0)

    piece = width // SPLIT
    spread = jnp.concatenate([rows[:8, j * piece : (j + 1) * piece] for j in range(SPLIT)], axis=0)
    outgoing = jnp.dot(place, spread.astype(jnp.bfloat16), preferred_element_type=jnp.float32)
    messages[...] = outgoing.astype(jnp.bfloat16).reshape(wide_count, MSG, piece)
    holder = w // sources
    slot = lax.rem(w, sources) * narrow_count + n

    def message_copy(target, at):
        return pltpu.make_async_remote_copy(
            src_ref=messages.at[target],
            dst_ref=messages_in.at[at],
            send_sem=msg_send.at[target],
            recv_sem=msg_recv.at[at],
            device_id=(target, holder),
            device_id_type=MESH,
        )

    local_message = pltpu.make_async_copy(
        messages.at[w], messages_in.at[slot], own_sem.at[2]
    )

    @pl.loop(1, wide_count)
    def _(k):
        message_copy(lax.rem(w + k, wide_count), slot).start()

    @pl.when(holder == n)
    def _():
        local_message.start()

    @pl.when(holder != n)
    def _():
        message_copy(w, slot).start()

    scores = factor * lax.dot_general(
        rows.astype(jnp.bfloat16), blocks[...], contract, preferred_element_type=jnp.float32
    )
    spot = lax.broadcasted_iota(jnp.int32, (MSG, 1), 0)
    valid = spot < per
    numbers = devices * old_rows + w * passages + n * per + spot
    picked += jnp.sum(jnp.where(valid & (numbers == chosen), scores, 0.0), axis=0, keepdims=True)
    masked = jnp.where(valid, scores, -jnp.inf)
    new_top = jnp.maximum(top, jnp.max(masked, axis=0, keepdims=True))
    mass = mass * jnp.exp(top - new_top) + jnp.sum(
        jnp.exp(masked - new_top), axis=0, keepdims=True
    )
    halves = count // 128
    stat = [v[:, h * 128 : (h + 1) * 128] for v in (new_top, mass, picked) for h in range(halves)]
    stat.append(jnp.zeros((8 - 3 * halves, 128), jnp.float32))
    stats[me] = jnp.concatenate(stat, axis=0)

    def stat_copy(sender, target):
        return pltpu.make_async_remote_copy(
            src_ref=stats.at[sender],
            dst_ref=stats.at[sender],
            send_sem=stat_send.at[target],
            recv_sem=stat_recv.at[sender],
            device_id=(target // narrow_count, lax.rem(target, narrow_count)),
            device_id_type=MESH,
        )

    @pl.loop(1, devices)
    def _(k):
        stat_copy(me, lax.rem(me + k, devices)).start()

    @pl.loop(0, sources)
    def _(a):
        @pl.loop(0, narrow_count)
        def _(b):
            at = a * narrow_count + b

            @pl.when((n * sources + a == w) & (b == n))
            def _():
                local_message.wait()

            @pl.when((n * sources + a != w) | (b != n))
            def _():
                message_copy(w, at).wait_recv()

    for a in range(sources):
        held = messages_in[a * narrow_count].astype(jnp.float32)
        for b in range(1, narrow_count):
            held += messages_in[a * narrow_count + b].astype(jnp.float32)
        index_ref[a] = jnp.concatenate(
            [held[j * capacity : (j + 1) * capacity] for j in range(SPLIT)], axis=1
        )

    @pl.loop(1, devices)
    def _(k):
        stat_copy(lax.rem(me + k, devices), me).wait_recv()

    every = stats[...]
    tops = every[:, :halves, :]
    largest = jnp.max(tops, axis=0)
    masses = jnp.sum(every[:, halves : 2 * halves, :] * jnp.exp(tops - largest[None]), axis=0)
    chosen_score = jnp.sum(every[:, 2 * halves : 3 * halves, :], axis=0)
    base = largest - chosen_score
    for t in range(steps):
        side = t % 2 * block
        losses_ref[0, t : t + 1, :] = base[t // 2 : t // 2 + 1, side : side + block]
        losses_ref[1, t : t + 1, :] = masses[t // 2 : t // 2 + 1, side : side + block]

    @pl.loop(1, wide_count)
    def _(k):
        target = lax.rem(w + k, wide_count)
        for copy in query_copies(w, target):
            copy.wait_send()
        message_copy(target, slot).wait_send()

    @pl.when(holder != n)
    def _():
        message_copy(w, slot).wait_send()

    for k in range(1, narrow_count):
        part_copy(n, lax.rem(n + k, narrow_count)).wait_send()

    @pl.loop(1, devices)
    def _(k):
        stat_copy(me, lax.rem(me + k, devices)).wait_send()


def local(
    tokens,
    ln_gain,
    gate_weight,
    up_weight,
    down_weight,
    out_gain,
    shard_ids,
    slab_old,
    queries,
    positives,
    owners,
):
    passages, seq, width = tokens.shape
    narrow_count = lax.axis_size("narrow")
    wide_count = lax.axis_size("wide")
    units = gate_weight.shape[1]
    steps, block = owners.shape[0], queries.shape[1]
    count = steps * block
    per = passages // narrow_count
    capacity = 2 * passages // wide_count
    sources = wide_count // narrow_count
    devices = wide_count * narrow_count
    groups = 8 // per
    lanes = width // groups
    piece = width // SPLIT
    chunks = -(-units // CHUNK)

    vmem = pl.BlockSpec(memory_space=pltpu.VMEM)
    anywhere = pl.BlockSpec(memory_space=pl.ANY)
    smem = pl.BlockSpec(memory_space=pltpu.SMEM)
    dma = pltpu.SemaphoreType.DMA
    flops = 4 * passages * seq * width * units + 2 * count * width * slab_old.shape[0]
    moved = 2 * width * (passages * seq + 3 * units + slab_old.shape[0])
    index_part, losses = pl.pallas_call(
        functools.partial(kernel, (passages, seq, wide_count, narrow_count, steps, block)),
        out_shape=(
            jax.ShapeDtypeStruct((sources, capacity, width), jnp.float32),
            jax.ShapeDtypeStruct((2, steps, block), jnp.float32),
        ),
        in_specs=[
            anywhere,
            vmem,
            vmem,
            anywhere,
            anywhere,
            anywhere,
            smem,
            anywhere,
            anywhere,
            vmem,
            smem,
        ],
        out_specs=(vmem, vmem),
        scratch_shapes=[
            pltpu.VMEM((passages * seq, width), jnp.bfloat16),
            pltpu.VMEM((units, width), jnp.bfloat16),
            pltpu.VMEM((units, width), jnp.bfloat16),
            pltpu.VMEM((units, width), jnp.bfloat16),
            pltpu.VMEM(slab_old.shape, jnp.bfloat16),
            pltpu.VMEM((wide_count, block, width), jnp.bfloat16),
            pltpu.VMEM((8, 2 * block), jnp.int32),
            pltpu.VMEM((wide_count, 8, 2 * block), jnp.int32),
            pltpu.VMEM((count, width), jnp.bfloat16),
            pltpu.VMEM((chunks, passages, CHUNK), jnp.float32),
            pltpu.VMEM((passages, width), jnp.float32),
            pltpu.VMEM((2 * passages, width), jnp.float32),
            pltpu.VMEM((narrow_count, 8, lanes), jnp.float32),
            pltpu.VMEM((narrow_count, 8, lanes), jnp.float32),
            pltpu.VMEM((wide_count, MSG, piece), jnp.bfloat16),
            pltpu.VMEM((sources * narrow_count, MSG, piece), jnp.bfloat16),
            pltpu.VMEM((devices, 8, 128), jnp.float32),
            dma((passages,)),
            dma((2, chunks)),
            dma((2,)),
            dma((3,)),
            dma((wide_count,)),
            dma((wide_count,)),
            dma((wide_count,)),
            dma((wide_count,)),
            dma((narrow_count,)),
            dma((narrow_count,)),
            dma((wide_count,)),
            dma((sources * narrow_count,)),
            dma((devices,)),
            dma((devices,)),
        ],
        compiler_params=pltpu.CompilerParams(
            collective_id=0, has_side_effects=True, vmem_limit_bytes=58 * 1024 * 1024
        ),
        cost_estimate=pl.CostEstimate(
            flops=flops, bytes_accessed=moved, transcendentals=passages * seq * units
        ),
    )(
        tokens.reshape(passages * seq, width),
        ln_gain,
        out_gain,
        gate_weight.T,
        up_weight.T,
        down_weight,
        shard_ids,
        slab_old,
        queries[0],
        positives,
        owners,
    )
    return index_part[None].astype(jnp.bfloat16), losses[0] + jnp.log(losses[1])


def solution(mesh):
    return jax.shard_map(
        local,
        mesh=mesh,
        in_specs=(
            P("wide", None, None),
            P(),
            P(None, "narrow"),
            P(None, "narrow"),
            P("narrow", None),
            P(),
            P("wide"),
            P(("wide", "narrow"), None),
            P("wide", None, None),
            P("wide", None),
            P(),
        ),
        out_specs=(P("wide", "narrow", None, None), P()),
        check_vma=False,
    )
```
